32 devices in a mesh: groups: 2 (over y), tensor: 4 (over z), dp: 4 (over x, core).
Axes of the slice: x: 2, y: 2, z: 4, core: 2. Of those that a mesh axis runs over, the one named last changes fastest.
Arguments:
- tokens: bfloat16 [512, 8192], P(('groups', 'tensor'), 'dp'), parts along dimension 0, may hold values from -6 to 6
- gate_code: bfloat16 [8192, 26624], P('dp', 'tensor'), may hold values from -8 to 7, as said below
- up_code: bfloat16 [8192, 26624], P('dp', 'tensor'), may hold values from -8 to 7, as said below
- down_code: bfloat16 [26624, 8192], P('tensor', 'dp'), may hold values from -8 to 7, as said below
- gate_scale: bfloat16 [64, 26624], P('dp', 'tensor'), may hold values from 0.0011825562 to 0.004760742
- up_scale: bfloat16 [64, 26624], P('dp', 'tensor'), may hold values from 0.0011825562 to 0.004760742
- down_scale: bfloat16 [208, 8192], P('tensor', 'dp'), may hold values from 0.0006599426 to 0.0026397705
- sign_bits: int32 [26624], P('tensor'), may hold values 0 or 1
Outputs:
- mixed: bfloat16 [512, 8192], P(('groups', 'tensor'), 'dp'), parts along dimension 0
The draws below stay inside these ranges and needn't reach their ends.
There are 2 independent parts, one for each index of `groups`. The reference program is written for one: setup_inputs(seed, part) draws one part's arguments, and reference() takes and returns one part's arrays. A program takes and returns all parts, laid end to end along the dimension named above; an argument that names none is the same for every part. Nothing has to cross between parts.
Inputs may be any that keep to these rules, and one draw needn't show every extreme that they name: `gate_code`: integer codes. `up_code`: integer codes. `down_code`: integer codes.
All inputs are finite; a program needn't handle non-finite values. No bound on the sum of `sign_bits` on one device may be relied on, other than what follows from the above.
Results may differ from the reference program's by a relative error of at most 0.02.
Values may be sent and summed in bfloat16 or wider, within the bound.
No kernel may reach another device: no remote copies, remote signals or barrier semaphores. Data moves between devices by JAX's collectives and lax.ppermute only.
A program may use at most 320 MiB of HBM per device.

```python
import math
import jax
import jax.numpy as jnp
from jax import lax

D = 8192
POW = 2048
FACTOR = 13
GROUP = 128
FF = 26624
ROWS = 256
IN_BLOCKS = 4
UNIT_BLOCKS = 4


def draw_gate_code(key, part):
    key = jax.random.fold_in(key, 11)
    return jax.random.randint(key, (D, FF), -8, 8, dtype=jnp.int32).astype(jnp.float32).astype(jnp.bfloat16)


def draw_up_code(key, part):
    key = jax.random.fold_in(key, 23)
    return jax.random.randint(key, (D, FF), -8, 8, dtype=jnp.int32).astype(jnp.float32).astype(jnp.bfloat16)


def draw_down_code(key, part):
    key = jax.random.fold_in(key, 37)
    return jax.random.randint(key, (FF, D), -8, 8, dtype=jnp.int32).astype(jnp.float32).astype(jnp.bfloat16)


def place_ends(drawn, stream_key, least, top_value):
    index_at = [jax.random.randint(jax.random.fold_in(stream_key, axis), (), 0, length) for axis, length in enumerate(drawn.shape)]
    main_axis = drawn.shape.index(max(drawn.shape))
    neighbour = index_at[:main_axis] + [(index_at[main_axis] + 1) % drawn.shape[main_axis]] + index_at[main_axis + 1:]
    return drawn.at[tuple(index_at)].set(least).at[tuple(neighbour)].set(top_value)


def block_levels(own_key, shape, shards, low, high):
    def one(position, parts):
        steps = jax.random.uniform(jax.random.fold_in(jax.random.fold_in(own_key, 6), position), (parts,), jnp.float32, low / len(shards), high / len(shards))
        return jnp.repeat(jnp.exp(steps), shape[position] // parts).reshape((-1,) + (1,) * (len(shape) - position - 1))

    factor_of = one(*shards[0])
    for cut in shards[1:]:
        factor_of = factor_of * one(*cut)
    return factor_of


def bell_draw(key, dims, scale, bound, split=(), kind=jnp.bfloat16):
    values = scale * jax.random.normal(key, dims, jnp.float32)
    if split:
        values = values * block_levels(key, dims, split, -0.22, 0.18)
    return jnp.clip(values, -bound, bound).astype(kind)


def setup_inputs(seed: int = 0, part: int = 0) -> dict:
    arg_keys = jax.random.split(jax.random.key(seed), 9)
    part_keys = jax.random.split(jax.random.fold_in(arg_keys[8], part), 9)
    tokens = bell_draw(part_keys[0], (ROWS, D), 1.0, 6.0, ((0, 4), (1, 4)))
    gate_code = draw_gate_code(jax.random.fold_in(arg_keys[8], 71), part)
    up_code = draw_up_code(jax.random.fold_in(arg_keys[8], 71), part)
    down_code = draw_down_code(jax.random.fold_in(arg_keys[8], 71), part)
    gate_scale = jnp.clip(jnp.exp(math.log(0.004760742) - 1.39272525 * jax.random.uniform(arg_keys[4], (D // GROUP, FF), jnp.float32) ** block_levels(arg_keys[4], (D // GROUP, FF), ((0, 4), (1, 4)), -0.2, 0.2)), 0.0011825562, 0.004760742).astype(jnp.bfloat16)
    up_scale = jnp.clip(jnp.exp(math.log(0.004760742) - 1.39272525 * jax.random.uniform(arg_keys[5], (D // GROUP, FF), jnp.float32) ** block_levels(arg_keys[5], (D // GROUP, FF), ((0, 4), (1, 4)), -0.2, 0.2)), 0.0011825562, 0.004760742).astype(jnp.bfloat16)
    down_scale = jnp.clip(jnp.exp(math.log(0.0026397705) - 1.3862944 * jax.random.uniform(arg_keys[6], (FF // GROUP, D), jnp.float32) ** block_levels(arg_keys[6], (FF // GROUP, D), ((0, 4), (1, 4)), -0.2, 0.2)), 0.0006599426, 0.0026397705).astype(jnp.bfloat16)
    sign_bits = place_ends((jax.random.randint(arg_keys[7], (FF,), 0, 2) < 1).astype(jnp.int32), jax.random.fold_in(arg_keys[7], 1), 0, 1)
    return dict(tokens=tokens, gate_code=gate_code, up_code=up_code, down_code=down_code, gate_scale=gate_scale, up_scale=up_scale, down_scale=down_scale, sign_bits=sign_bits)


def sylvester(order):
    index = jnp.arange(order, dtype=jnp.int32)
    common = jnp.bitwise_and(index[:, None], index[None, :])
    parity = jnp.zeros_like(common)
    for bit_index in range(max(order.bit_length() - 1, 0)):
        parity = parity + jnp.bitwise_and(jnp.right_shift(common, bit_index), 1)
    return (1 - 2 * (parity % 2)).astype(jnp.float32)


def dequant(codes, scales):
    row_count, col_count = codes.shape
    grouped = codes.reshape(scales.shape[0], row_count // scales.shape[0], col_count).astype(jnp.float32)
    product = grouped * scales.astype(jnp.float32)[:, None, :]
    return product.reshape(row_count, col_count).astype(jnp.bfloat16)


def reference(tokens, gate_code, up_code, down_code, gate_scale, up_scale, down_scale, sign_bits):
    row_count = tokens.shape[0]
    feat_block = D // IN_BLOCKS
    pre = jnp.zeros((row_count, 2 * FF), jnp.float32)
    for block in range(IN_BLOCKS):
        low = block * feat_block
        high = low + feat_block
        glow = low // GROUP
        ghigh = high // GROUP
        gate_w = dequant(gate_code[low:high], gate_scale[glow:ghigh])
        up_w = dequant(up_code[low:high], up_scale[glow:ghigh])
        gate_up = jnp.concatenate([gate_w, up_w], axis=1)
        term = jnp.dot(tokens[:, low:high], gate_up, preferred_element_type=jnp.float32)
        term = lax.optimization_barrier(term.astype(jnp.bfloat16))
        pre = pre + term.astype(jnp.float32)
    sign_values = 2.0 * sign_bits.astype(jnp.float32) - 1.0
    hidden = jax.nn.silu(pre[:, :FF]) * pre[:, FF:] * sign_values[None, :]
    levels = POW.bit_length() - 1
    first = 2 ** (levels // 2)
    second = POW // first
    hadamard_a = sylvester(first)
    hadamard_b = sylvester(second)
    shaped = hidden.reshape(row_count, first, second, FACTOR)
    shaped = jnp.einsum('ab,rbjc->rajc', hadamard_a, shaped, precision=lax.Precision.HIGHEST)
    shaped = jnp.einsum('jk,rakc->rajc', hadamard_b, shaped, precision=lax.Precision.HIGHEST)
    rotated = (shaped.reshape(row_count, FF) * (POW ** -0.5)).astype(jnp.bfloat16)
    unit_block = FF // UNIT_BLOCKS
    result = jnp.zeros((row_count, D), jnp.float32)
    for block in range(UNIT_BLOCKS):
        low = block * unit_block
        high = low + unit_block
        down_w = dequant(down_code[low:high], down_scale[low // GROUP:high // GROUP])
        term = jnp.dot(rotated[:, low:high], down_w, preferred_element_type=jnp.float32)
        term = lax.optimization_barrier(term.astype(jnp.bfloat16))
        result = result + term.astype(jnp.float32)
    return result.astype(jnp.bfloat16)
```

```python
import functools

import jax
import jax.numpy as jnp
import numpy as np
from jax import lax
from jax.experimental import pallas as pl
from jax.experimental.pallas import tpu as pltpu
from jax.sharding import PartitionSpec as P

POW = 2048
FACTOR = 13
LOW = 128
VMEM_LIMIT = 56 * 2**20


def bits_of(size):
    return size.bit_length() - 1


def swap(shard, axis, bit):
    return lax.ppermute(shard, axis, [(i, i ^ 1 << bit) for i in range(lax.axis_size(axis))])


def shift(shard, axis):
    size = lax.axis_size(axis)
    return lax.ppermute(shard, axis, [(i, (i + 1) % size) for i in range(size)])


def reversed_bits(value, bits):
    return sum((value >> i & 1) << (bits - 1 - i) for i in range(bits))


def params(**more):
    return pltpu.CompilerParams(vmem_limit_bytes=VMEM_LIMIT, **more)


def low_rotation():
    order = np.arange(LOW)
    common = order[:, None] & order[None, :]
    parity = np.zeros_like(common)
    for bit in range(bits_of(LOW)):
        parity ^= common >> bit & 1
    return np.kron(1 - 2 * parity, np.eye(FACTOR)).astype(jnp.bfloat16)


def scaled(codes, scales):
    depth, cols = codes.shape
    groups = scales.shape[0]
    product = codes.astype(jnp.float32).reshape(groups, depth // groups, cols) * scales[:, None, :]
    return product.astype(jnp.bfloat16).reshape(depth, cols)


def gate_up_kernel(peers, pieces, *refs):
    token_refs = refs[:peers]
    gate_ref, up_ref, gate_scale_ref, up_scale_ref, keep_ref, send_ref, rows_ref, scale_ref, total_ref = refs[peers:]
    step = pl.program_id(0)
    depth = gate_ref.shape[0]
    part = token_refs[0].shape[0]
    steps = rows_ref.shape[0]
    groups = scale_ref.shape[1] // steps

    @pl.when(step == 0)
    def _():
        place = lax.axis_index("tensor")
        for hop, token_ref in enumerate(token_refs):
            row = pl.multiple_of(lax.rem(place + peers - hop, peers) * part, part)
            for index in range(steps):
                rows_ref[index, pl.ds(row, part), :] = token_ref[:, index * depth : (index + 1) * depth]
        scale_ref[0] = gate_scale_ref[...].astype(jnp.float32)
        scale_ref[1] = up_scale_ref[...].astype(jnp.float32)
        total_ref[...] = jnp.zeros_like(total_ref)

    rows = rows_ref[step]
    first = pl.multiple_of(step * groups, groups)
    for side, code_ref in enumerate((gate_ref, up_ref)):
        weight = scaled(code_ref[...], scale_ref[side, pl.ds(first, groups), :])
        total_ref[side] += jnp.dot(rows, weight, preferred_element_type=jnp.float32)

    @pl.when(step == steps - 1)
    def _():
        own = lax.axis_index("dp")
        share = total_ref.shape[1] // pieces
        for piece in range(pieces):
            block = own ^ reversed_bits(piece, bits_of(pieces))
            row = pl.multiple_of(block * share, share)
            out_ref = keep_ref if piece < pieces // 2 else send_ref
            out_ref[piece % (pieces // 2)] = total_ref[:, pl.ds(row, share), :].astype(jnp.bfloat16)


def gate_up(token_parts, gate_code, up_code, gate_scale, up_scale, chunk, width):
    peers = len(token_parts)
    pieces = lax.axis_size("dp")
    part, features = token_parts[0].shape
    row_count = part * peers
    depth = min(features, 1024)
    steps = features // depth
    groups = gate_scale.shape[0]
    share = row_count // pieces
    code_spec = pl.BlockSpec((depth, width), lambda k: (k, chunk))
    scale_spec = pl.BlockSpec((groups, width), lambda k: (0, chunk))
    out = jax.ShapeDtypeStruct((pieces // 2, 2, share, width), jnp.bfloat16)
    out_spec = pl.BlockSpec(out.shape, lambda k: (0, 0, 0, 0))
    return pl.pallas_call(
        functools.partial(gate_up_kernel, peers, pieces),
        grid=(steps,),
        in_specs=[pl.BlockSpec((part, features), lambda k: (0, 0))] * peers
        + [code_spec, code_spec, scale_spec, scale_spec],
        out_specs=[out_spec, out_spec],
        out_shape=[out, out],
        scratch_shapes=[
            pltpu.VMEM((steps, row_count, depth), jnp.bfloat16),
            pltpu.VMEM((2, groups, width), jnp.float32),
            pltpu.VMEM((2, row_count, width), jnp.float32),
        ],
        compiler_params=params(),
        cost_estimate=pl.CostEstimate(
            flops=4 * row_count * features * width, bytes_accessed=4 * features * width, transcendentals=0
        ),
        name=f"gate_up_{chunk}",
    )(*token_parts, gate_code, up_code, gate_scale, up_scale)


def hidden_kernel(*refs):
    term_refs, (sign_ref, rotation_ref, out_ref) = refs[:-3], refs[-3:]
    total = sum(ref[0].astype(jnp.float32) for ref in term_refs)
    gate, up = total[0], total[1]
    hidden = gate / (1.0 + jnp.exp(-gate)) * up * sign_ref[0]
    out_ref[...] = jnp.dot(
        hidden.astype(jnp.bfloat16), rotation_ref[...], preferred_element_type=jnp.float32
    ).astype(jnp.bfloat16)


def hidden_of(terms, signs, rotation, chunk):
    _, _, share, width = terms[0].shape
    return pl.pallas_call(
        hidden_kernel,
        grid=(1,),
        in_specs=[pl.BlockSpec((1, 2, share, width), lambda k: (0, 0, 0, 0))] * len(terms)
        + [pl.BlockSpec((1, 1, width), lambda k: (chunk, 0, 0)), pl.BlockSpec((width, width), lambda k: (0, 0))],
        out_specs=pl.BlockSpec((share, width), lambda k: (0, 0)),
        out_shape=jax.ShapeDtypeStruct((share, width), jnp.bfloat16),
        compiler_params=params(),
        cost_estimate=pl.CostEstimate(
            flops=2 * share * width * width, bytes_accessed=2 * width * width, transcendentals=share * width
        ),
        name=f"hidden_{chunk}",
    )(*terms, signs, rotation)


def down_kernel(chunks, pieces, peers, *refs):
    part_refs = refs[: chunks * pieces]
    code_ref, scale_in_ref, out_ref, rows_ref, scale_ref, total_ref = refs[chunks * pieces :]
    step = pl.program_id(0)
    share, width = part_refs[0].shape
    row_count = share * pieces
    groups = scale_in_ref.shape[0] // chunks

    @pl.when(step == 0)
    def _():
        own = lax.axis_index("dp")
        place = lax.axis_index("tensor")
        part = row_count // peers
        for piece in range(pieces):
            block = own ^ reversed_bits(piece, bits_of(pieces))
            row = block * share
            turn = lax.rem(place + 2 * peers - 1 - row // part, peers)
            row = pl.multiple_of(turn * part + lax.rem(row, part), share)
            values = [part_refs[chunk * pieces + piece][...].astype(jnp.float32) for chunk in range(chunks)]
            gap = 1
            while gap < chunks:
                for low in range(chunks):
                    if not low & gap:
                        left, right = values[low], values[low | gap]
                        values[low], values[low | gap] = left + right, left - right
                gap *= 2
            for chunk in range(chunks):
                rows_ref[chunk, pl.ds(row, share), :] = (values[chunk] * POW**-0.5).astype(jnp.bfloat16)
        scales = scale_in_ref[...].astype(jnp.float32)
        for chunk in range(chunks):
            scale_ref[chunk, :groups, :] = scales[chunk * groups : (chunk + 1) * groups]
        total_ref[...] = jnp.zeros_like(total_ref)

    weight = scaled(code_ref[...], scale_ref[step, :groups, :])
    total_ref[...] += jnp.dot(rows_ref[step], weight, preferred_element_type=jnp.float32)

    @pl.when(step == chunks - 1)
    def _():
        out_ref[...] = total_ref[...].astype(jnp.bfloat16).reshape(out_ref.shape)


def down(parts, down_code, down_scale, column, columns):
    chunks, pieces = len(parts), len(parts[0])
    peers = lax.axis_size("tensor")
    share, width = parts[0][0].shape
    row_count = share * pieces
    groups = down_scale.shape[0]
    room = -(-groups // chunks // 8) * 8
    out = jax.ShapeDtypeStruct((peers, row_count // peers, columns), jnp.bfloat16)
    return pl.pallas_call(
        functools.partial(down_kernel, chunks, pieces, peers),
        grid=(chunks,),
        in_specs=[pl.BlockSpec((share, width), lambda k: (0, 0))] * (chunks * pieces)
        + [
            pl.BlockSpec((width, columns), lambda k: (k, column)),
            pl.BlockSpec((groups, columns), lambda k: (0, column)),
        ],
        out_specs=pl.BlockSpec(out.shape, lambda k: (0, 0, 0)),
        out_shape=out,
        scratch_shapes=[
            pltpu.VMEM((chunks, row_count, width), jnp.bfloat16),
            pltpu.VMEM((chunks, room, columns), jnp.float32),
            pltpu.VMEM((row_count, columns), jnp.float32),
        ],
        compiler_params=params(),
        cost_estimate=pl.CostEstimate(
            flops=2 * row_count * chunks * width * columns,
            bytes_accessed=2 * chunks * width * columns,
            transcendentals=0,
        ),
        name=f"down_{column}",
    )(*[part for row in parts for part in row], down_code, down_scale)


def add(*terms):
    return sum(term.astype(jnp.float32) for term in terms).astype(jnp.bfloat16)


def halved(keep, send):
    terms = [keep]
    for bit in range(bits_of(lax.axis_size("dp"))):
        if bit:
            half = terms[0].shape[0] // 2
            send = add(*[term[half : 2 * half] for term in terms])
            terms = [term[:half] for term in terms] if half > 1 else terms
        terms = terms + [swap(send, "dp", bit)]
    return terms


def rotated_over(hidden, axis):
    place = lax.axis_index(axis)
    for bit in range(bits_of(lax.axis_size(axis))):
        sign = (1 - 2 * (place >> bit & 1)).astype(jnp.float32)
        partner = swap(hidden, axis, bit)
        hidden = (partner.astype(jnp.float32) + sign * hidden.astype(jnp.float32)).astype(jnp.bfloat16)
    return hidden


def doubled(hidden, axis):
    parts = [hidden]
    for bit in reversed(range(bits_of(lax.axis_size(axis)))):
        parts = parts + [swap(part, axis, bit) for part in parts]
    return parts


def on_device(tokens, gate_code, up_code, down_code, gate_scale, up_scale, down_scale, sign_bits):
    peers = lax.axis_size("tensor")
    width = LOW * FACTOR
    chunks = gate_code.shape[1] // width
    rotation = jnp.asarray(low_rotation())
    signs = (2.0 * sign_bits.astype(jnp.float32) - 1.0).reshape(chunks, 1, width)

    token_parts = [tokens]
    for _ in range(peers - 1):
        token_parts.append(shift(token_parts[-1], "tensor"))

    parts = []
    for chunk in range(chunks):
        keep, send = gate_up(token_parts, gate_code, up_code, gate_scale, up_scale, chunk, width)
        hidden = hidden_of(halved(keep, send), signs, rotation, chunk)
        parts.append(doubled(rotated_over(hidden, "tensor"), "dp"))

    features = down_code.shape[1]
    halves = 2
    columns = features // halves
    results = []
    for column in range(halves):
        terms = down(parts, down_code, down_scale, column, columns)
        total = terms[0]
        for hop in range(1, peers):
            total = add(shift(total, "tensor"), terms[hop])
        results.append(total)
    return jnp.concatenate(results, axis=1)


def solution(mesh):
    in_specs = (
        P(("groups", "tensor"), "dp"),
        P("dp", "tensor"),
        P("dp", "tensor"),
        P("tensor", "dp"),
        P("dp", "tensor"),
        P("dp", "tensor"),
        P("tensor", "dp"),
        P("tensor"),
    )
    out_specs = P(("groups", "tensor"), "dp")
    return jax.shard_map(
        on_device, mesh=mesh, in_specs=in_specs, out_specs=out_specs, check_vma=False
    )
```

```python
import functools

import jax
import jax.numpy as jnp
import numpy as np
from jax import lax
from jax.experimental import pallas as pl
from jax.experimental.pallas import tpu as pltpu
from jax.sharding import PartitionSpec as P

POW = 2048
FACTOR = 13
LOW = 128
SMALL = 16
TILE = 512
AHEAD = 3
VMEM_LIMIT = 56 * 2**20


def bits_of(size):
    return size.bit_length() - 1


def swap(shard, axis, bit):
    return lax.ppermute(shard, axis, [(i, i ^ 1 << bit) for i in range(lax.axis_size(axis))])


def shift(shard, axis, step=1):
    size = lax.axis_size(axis)
    return lax.ppermute(shard, axis, [(i, (i + step) % size) for i in range(size)])


def reversed_bits(value, bits):
    return sum((value >> i & 1) << (bits - 1 - i) for i in range(bits))


def params(**more):
    return pltpu.CompilerParams(vmem_limit_bytes=VMEM_LIMIT, **more)


def matrix_part():
    order = np.arange(SMALL)
    common = order[:, None] & order[None, :]
    parity = np.zeros_like(common)
    for bit in range(bits_of(SMALL)):
        parity ^= common >> bit & 1
    return np.kron(1 - 2 * parity, np.eye(FACTOR)).astype(jnp.bfloat16)


def butterflies(values):
    values = list(values)
    gap = 1
    while gap < len(values):
        for low in range(len(values)):
            if not low & gap:
                left, right = values[low], values[low | gap]
                values[low], values[low | gap] = left + right, left - right
        gap *= 2
    return values


def scaled(codes, scales):
    depth, cols = codes.shape
    groups = scales.shape[0]
    product = codes.astype(jnp.float32).reshape(groups, depth // groups, cols) * scales[:, None, :]
    return product.astype(jnp.bfloat16).reshape(depth, cols)


def fold_kernel(chunks, blocks, first, *refs):
    code_refs, (scale_in_ref, out_ref, scale_ref) = refs[:chunks], refs[chunks:]
    step = pl.program_id(0)

    @pl.when(step == 0)
    def _():
        scale_ref[...] = scale_in_ref[...].astype(jnp.float32)

    values = [
        code_refs[chunk][...].astype(jnp.float32) * scale_ref[pl.ds(chunk * blocks + first + step, 1), :]
        for chunk in range(chunks)
    ]
    for chunk, value in enumerate(butterflies(values)):
        out_ref[chunk] = value.astype(jnp.bfloat16)


def folded(down_code, down_scale, chunks, first, count):
    units, features = down_code.shape
    groups = down_scale.shape[0]
    blocks = groups // chunks
    depth = units // groups

    def code_spec(chunk):
        return pl.BlockSpec((depth, features), lambda k: (chunk * blocks + first + k, 0))

    return pl.pallas_call(
        functools.partial(fold_kernel, chunks, blocks, first),
        grid=(count,),
        in_specs=[code_spec(chunk) for chunk in range(chunks)]
        + [pl.BlockSpec((groups, features), lambda k: (0, 0))],
        out_specs=pl.BlockSpec((chunks, depth, features), lambda k: (0, k, 0)),
        out_shape=jax.ShapeDtypeStruct((chunks, count * depth, features), jnp.bfloat16),
        scratch_shapes=[pltpu.VMEM((groups, features), jnp.float32)],
        compiler_params=params(),
        cost_estimate=pl.CostEstimate(
            flops=0, bytes_accessed=4 * chunks * count * depth * features, transcendentals=0
        ),
        name=f"fold_down_{first}",
    )(*[down_code] * chunks, down_scale)


def tiles_of(width):
    return [(low, min(TILE, width - low)) for low in range(0, width, TILE)]


def gate_up_kernel(parts, peers, pieces, chunk, *refs):
    token_refs = refs[:parts]
    code_refs = refs[parts : parts + 2]
    scale_refs = refs[parts + 2 : parts + 4]
    keep_ref, send_ref, rows_ref, codes_ref, terms_ref, arrived, done, left = refs[parts + 4 :]
    part = token_refs[0].shape[0]
    half, _, share, width = keep_ref.shape
    tiles = [(side, low, size) for side in range(2) for low, size in tiles_of(width)]

    def fetch(index):
        side, low, size = tiles[index]
        return pltpu.make_async_copy(
            code_refs[side].at[:, pl.ds(chunk * width + low, size)],
            codes_ref.at[side, :, pl.ds(low, size)],
            done.at[index],
        )

    def leave(index, which):
        side, low, size = tiles[index]
        return pltpu.make_async_copy(
            terms_ref.at[pl.ds(which * half, half), side, :, pl.ds(low, size)],
            (keep_ref, send_ref)[which].at[:, side, :, pl.ds(low, size)],
            left.at[index, which],
        )

    place = lax.axis_index("tensor")
    own = lax.axis_index("dp")
    piece_bits = bits_of(pieces)
    unit = min(part, share)
    fetch(0).start()
    placed = []
    for hop in range(peers):
        base = lax.rem(place + peers - hop, peers) * part
        for low in range(0, part, unit):
            row = base + low
            mixed = (row // share) ^ own
            piece = sum((mixed >> bit & 1) << (piece_bits - 1 - bit) for bit in range(piece_bits))
            slot = pl.multiple_of(piece * share + lax.rem(row, share), unit)

            def put(index, low=low, slot=slot, number=len(placed)):
                return pltpu.make_async_copy(
                    token_refs[index].at[pl.ds(low, unit), :],
                    rows_ref.at[pl.ds(slot, unit), :],
                    arrived.at[number],
                )

            placed.append(put(hop))
            if parts > peers and hop == peers // 2:
                pl.when(place < peers // 2)(put(hop).start)
                pl.when(place >= peers // 2)(put(parts - 1).start)
            else:
                put(hop).start()
    for index in range(1, min(AHEAD, len(tiles))):
        fetch(index).start()
    for copy in placed:
        copy.wait()

    for index, (side, low, size) in enumerate(tiles):
        if index + AHEAD < len(tiles):
            fetch(index + AHEAD).start()
        fetch(index).wait()
        cols = slice(low, low + size)
        weight = scaled(codes_ref[side, :, cols], scale_refs[side][:, cols].astype(jnp.float32))
        terms = jnp.dot(rows_ref[...], weight, preferred_element_type=jnp.float32).astype(jnp.bfloat16)
        for piece in range(pieces):
            terms_ref[piece, side, :, cols] = terms[piece * share : (piece + 1) * share]
        for which in range(2):
            leave(index, which).start()
    for index in range(len(tiles)):
        for which in range(2):
            leave(index, which).wait()


def gate_up(token_parts, gate_code, up_code, gate_scale, up_scale, chunk, width):
    peers = lax.axis_size("tensor")
    pieces = lax.axis_size("dp")
    part, features = token_parts[0].shape
    row_count = part * peers
    share = row_count // pieces
    groups = gate_scale.shape[0]
    count = 2 * len(tiles_of(width))
    out = jax.ShapeDtypeStruct((pieces // 2, 2, share, width), jnp.bfloat16)
    anywhere = pl.BlockSpec(memory_space=pl.ANY)
    return pl.pallas_call(
        functools.partial(gate_up_kernel, len(token_parts), peers, pieces, chunk),
        grid=(1,),
        in_specs=[anywhere] * (len(token_parts) + 2) + [pl.BlockSpec((groups, width), lambda k: (0, chunk))] * 2,
        out_specs=[anywhere, anywhere],
        out_shape=[out, out],
        scratch_shapes=[
            pltpu.VMEM((row_count, features), jnp.bfloat16),
            pltpu.VMEM((2, features, width), jnp.bfloat16),
            pltpu.VMEM((pieces, 2, share, width), jnp.bfloat16),
            pltpu.SemaphoreType.DMA((row_count // min(part, share),)),
            pltpu.SemaphoreType.DMA((count,)),
            pltpu.SemaphoreType.DMA((count, 2)),
        ],
        compiler_params=params(),
        cost_estimate=pl.CostEstimate(
            flops=4 * row_count * features * width, bytes_accessed=4 * features * width, transcendentals=0
        ),
        name=f"gate_up_{chunk}",
    )(*token_parts, gate_code, up_code, gate_scale, up_scale)


def hidden_kernel(count, *refs):
    sign_ref, rotation_ref, out_ref = refs[count:]
    total = sum(ref[0].astype(jnp.float32) for ref in refs[:count])
    gate, up = total[0], total[1]
    hidden = gate / (1.0 + jnp.exp(-gate)) * up * sign_ref[0]
    share, width = out_ref.shape
    small = rotation_ref.shape[0]
    slices = butterflies(hidden[:, low : low + small] for low in range(0, width, small))
    stacked = jnp.concatenate(slices, axis=0).astype(jnp.bfloat16)
    turned = jnp.dot(stacked, rotation_ref[...], preferred_element_type=jnp.float32) * POW**-0.5
    turned = [turned[index * share : (index + 1) * share] for index in range(len(slices))]
    out_ref[...] = jnp.concatenate(turned, axis=1).astype(jnp.bfloat16)


def hidden_of(terms, signs, rotation, chunk):
    _, _, share, width = terms[0].shape
    small = rotation.shape[0]
    return pl.pallas_call(
        functools.partial(hidden_kernel, len(terms)),
        grid=(1,),
        in_specs=[pl.BlockSpec((1, 2, share, width), lambda k: (0, 0, 0, 0))] * len(terms)
        + [pl.BlockSpec((1, 1, width), lambda k: (chunk, 0, 0)), pl.BlockSpec((small, small), lambda k: (0, 0))],
        out_specs=pl.BlockSpec((share, width), lambda k: (0, 0)),
        out_shape=jax.ShapeDtypeStruct((share, width), jnp.bfloat16),
        compiler_params=params(),
        cost_estimate=pl.CostEstimate(
            flops=2 * share * width * small, bytes_accessed=2 * share * width * 7, transcendentals=share * width
        ),
        name=f"hidden_{chunk}",
    )(*terms, signs, rotation)


def down_kernel(chunks, pieces, peers, sums, weights, *refs):
    part_refs = refs[: chunks * pieces]
    weight_refs = refs[chunks * pieces : chunks * (pieces + weights)]
    sum_refs = refs[chunks * (pieces + weights) : chunks * (pieces + weights) + sums]
    out_ref, rows_ref = refs[chunks * (pieces + weights) + sums :]
    share = part_refs[0].shape[0]
    row_count = share * pieces

    @pl.when(pl.program_id(0) == 0)
    def _():
        own = lax.axis_index("dp")
        place = lax.axis_index("tensor")
        part = row_count // peers
        for piece in range(pieces):
            block = own ^ reversed_bits(piece, bits_of(pieces))
            row = block * share
            turn = lax.rem(place + 2 * peers - 1 - row // part, peers)
            row = pl.multiple_of(turn * part + lax.rem(row, part), share)
            for chunk in range(chunks):
                rows_ref[chunk, pl.ds(row, share), :] = part_refs[chunk * pieces + piece][...]

    total = None
    for chunk in range(chunks):
        low = 0
        for weight_ref in weight_refs[chunk * weights : (chunk + 1) * weights]:
            high = low + weight_ref.shape[1]
            term = jnp.dot(rows_ref[chunk, :, low:high], weight_ref[0], preferred_element_type=jnp.float32)
            total = term if total is None else total + term
            low = high
    total = total.reshape(out_ref.shape)
    for sum_ref in sum_refs:
        total = total + sum_ref[...]
    out_ref[...] = total.astype(out_ref.dtype)


def down(parts, weights, sums, chunk, column, columns, tile, kind):
    peers = lax.axis_size("tensor")
    chunks, pieces = len(parts), len(parts[0])
    share, width = parts[0][0].shape
    row_count = share * pieces
    part = row_count // peers
    start = column * columns // tile

    def weight_spec(weight, index):
        return pl.BlockSpec((1, weight.shape[1], tile), lambda k: (index, 0, start + k))

    return pl.pallas_call(
        functools.partial(down_kernel, chunks, pieces, peers, len(sums), len(weights)),
        grid=(columns // tile,),
        in_specs=[pl.BlockSpec((share, width), lambda k: (0, 0))] * (chunks * pieces)
        + [weight_spec(weight, chunk + index) for index in range(chunks) for weight in weights]
        + [pl.BlockSpec((peers, part, tile), lambda k: (0, 0, start + k))] * len(sums),
        out_specs=pl.BlockSpec((peers, part, tile), lambda k: (0, 0, k)),
        out_shape=jax.ShapeDtypeStruct((peers, part, columns), kind),
        scratch_shapes=[pltpu.VMEM((chunks, row_count, width), jnp.bfloat16)],
        compiler_params=params(),
        cost_estimate=pl.CostEstimate(
            flops=2 * row_count * chunks * width * columns,
            bytes_accessed=2 * chunks * width * columns,
            transcendentals=0,
        ),
        name=f"down_{chunk}_{column}",
    )(*[piece for row in parts for piece in row], *weights * chunks, *sums)


def add(*terms):
    return sum(term.astype(jnp.float32) for term in terms).astype(jnp.bfloat16)


class Order:
    def __init__(self):
        self.last = None

    def __call__(self, step, operands):
        if self.last is not None:
            operands, _ = lax.optimization_barrier((operands, self.last))
        result = step(operands)
        self.last = jax.tree.leaves(result)[0]
        return result

    def land(self, value):
        value, self.last = lax.optimization_barrier((value, self.last))
        return value


def upper(terms):
    half = terms[0].shape[0] // 2
    return add(*[term[half : 2 * half] for term in terms])


def lower(terms):
    half = terms[0].shape[0] // 2
    return [term[:half] for term in terms] if half > 1 else terms


def doubled(hidden, axis):
    parts = [hidden]
    for bit in reversed(range(bits_of(lax.axis_size(axis)))):
        parts = parts + [swap(part, axis, bit) for part in parts]
    return parts


def on_device(tokens, gate_code, up_code, down_code, gate_scale, up_scale, down_scale, sign_bits):
    peers = lax.axis_size("tensor")
    dp_bits = bits_of(lax.axis_size("dp"))
    turns = bits_of(peers)
    width = LOW * FACTOR
    chunks = gate_code.shape[1] // width
    rotation = jnp.asarray(matrix_part())
    signs = (2.0 * sign_bits.astype(jnp.float32) - 1.0).reshape(chunks, 1, width)
    place = lax.axis_index("tensor")
    features = down_code.shape[1]
    blocks = down_scale.shape[0] // chunks
    order = Order()
    weights = []
    all_terms = {}
    hiddens = {}
    parts = {}

    def fold(count):
        first = sum(weight.shape[1] for weight in weights) * chunks * down_scale.shape[0] // down_code.shape[0]
        first //= chunks
        weights.append(order(lambda codes: folded(codes, down_scale, chunks, first, count), down_code))

    def start_terms(chunk):
        keep, send = order(
            lambda ts: gate_up(ts, gate_code, up_code, gate_scale, up_scale, chunk, width), token_parts
        )
        all_terms[chunk] = [keep, swap(send, "dp", 0)]

    def pass_terms(chunk, bit=1):
        terms = all_terms[chunk]
        send = order(upper, terms)
        all_terms[chunk] = lower(terms) + [swap(send, "dp", bit)]

    def finish_terms(chunk):
        hidden = order(lambda ts: hidden_of(ts, signs, rotation, chunk), all_terms[chunk])
        hiddens[chunk] = hidden, swap(hidden, "tensor", 0)

    def turn(chunk, bit):
        sign = (1 - 2 * (place >> bit & 1)).astype(jnp.float32)
        hidden = order(lambda pair: add(pair[1], sign * pair[0].astype(jnp.float32)), hiddens[chunk])
        if bit + 1 < turns:
            hiddens[chunk] = hidden, swap(hidden, "tensor", bit + 1)
        else:
            parts[chunk] = doubled(hidden, "dp")

    def product(first, count, sums, column, columns, kind):
        given = [parts[chunk] for chunk in range(first, first + count)]
        tile = min(columns, 512)
        return order(lambda ps: down(ps, weights, sums, first, column, columns, tile, kind), given)

    def finish(first, count, sums, halves=2):
        columns = features // halves
        terms, totals = [], []
        for column in range(halves):
            terms.append(product(first, count, sums, column, columns, jnp.bfloat16))
            totals.append(shift(terms[-1][0], "tensor"))
        for hop in range(1, peers):
            for column in range(halves):
                totals[column] = order(lambda pair: add(*pair), (totals[column], terms[column][hop]))
                if hop < peers - 1:
                    totals[column] = shift(totals[column], "tensor")
        return jnp.concatenate(totals, axis=1)

    if peers == 4:
        before = shift(tokens, "tensor")
        behind = shift(tokens, "tensor", -1)
        fold(blocks // 3)
        before, behind, weights[0] = lax.optimization_barrier((before, behind, weights[0]))
        far_low = lax.ppermute(behind, "tensor", [(1, 0), (2, 1)])
        far_high = lax.ppermute(before, "tensor", [(1, 2), (2, 3)])
        token_parts = [tokens, before, far_low, behind, far_high]
        fold(blocks // 3)
    else:
        token_parts = [tokens]
        for _ in range(peers - 1):
            token_parts.append(shift(token_parts[-1], "tensor"))
    rest = blocks - sum(weight.shape[1] for weight in weights) * down_scale.shape[0] // down_code.shape[0]

    def land_terms(chunk):
        all_terms[chunk][-1] = order.land(all_terms[chunk][-1])

    def land_turn(chunk):
        hidden, partner = hiddens[chunk]
        hiddens[chunk] = hidden, order.land(partner)

    def land_parts(chunk):
        parts[chunk][1:] = order.land(parts[chunk][1:])

    if chunks == 4 and dp_bits == 2 and turns == 2:
        start_terms(0)
        start_terms(1)
        land_terms(0)
        pass_terms(0)
        start_terms(2)
        land_terms(0)
        land_terms(1)
        pass_terms(1)
        finish_terms(0)
        start_terms(3)
        land_turn(0)
        land_terms(1)
        land_terms(2)
        pass_terms(2)
        turn(0, 0)
        finish_terms(1)
        land_terms(3)
        pass_terms(3)
        fold(rest // 2)
        land_turn(1)
        turn(1, 0)
        land_terms(2)
        finish_terms(2)
        land_turn(0)
        turn(0, 1)
        fold(rest - rest // 2)
        land_turn(2)
        land_terms(3)
        finish_terms(3)
        turn(2, 0)
        land_turn(1)
        turn(1, 1)
        land_turn(3)
        turn(3, 0)
        land_parts(0)
        land_parts(1)
        sums = [product(0, 2, [], 0, features, jnp.float32)]
        land_turn(2)
        turn(2, 1)
        land_turn(3)
        turn(3, 1)
        land_parts(2)
        sums = [product(2, 1, sums, 0, features, jnp.float32)]
        return finish(3, 1, sums)
    fold(rest)
    for chunk in range(chunks):
        start_terms(chunk)
        for bit in range(1, dp_bits):
            pass_terms(chunk, bit)
        finish_terms(chunk)
        for bit in range(turns):
            turn(chunk, bit)
    return finish(0, chunks, [])


def solution(mesh):
    in_specs = (
        P(("groups", "tensor"), "dp"),
        P("dp", "tensor"),
        P("dp", "tensor"),
        P("tensor", "dp"),
        P("dp", "tensor"),
        P("dp", "tensor"),
        P("tensor", "dp"),
        P("tensor"),
    )
    out_specs = P(("groups", "tensor"), "dp")
    return jax.shard_map(
        on_device, mesh=mesh, in_specs=in_specs, out_specs=out_specs, check_vma=False
    )
```

```python
import functools

import jax
import jax.numpy as jnp
import numpy as np
from jax import lax
from jax.experimental import pallas as pl
from jax.experimental.pallas import tpu as pltpu
from jax.sharding import PartitionSpec as P

POW = 2048
FACTOR = 13
LOW = 128
SMALL = 16
FOLD = 8
DEPTH = 1024
AHEAD = 2
VMEM_LIMIT = 32 * 2**20


def bits_of(size):
    return size.bit_length() - 1


def swap(shard, axis, bit):
    return lax.ppermute(shard, axis, [(i, i ^ 1 << bit) for i in range(lax.axis_size(axis))])


def shift(shard, axis, step=1):
    size = lax.axis_size(axis)
    return lax.ppermute(shard, axis, [(i, (i + step) % size) for i in range(size)])


def reversed_bits(value, bits):
    return sum((value >> i & 1) << (bits - 1 - i) for i in range(bits))


def params(**more):
    return pltpu.CompilerParams(vmem_limit_bytes=VMEM_LIMIT, **more)


def matrix_part():
    order = np.arange(SMALL)
    common = order[:, None] & order[None, :]
    parity = np.zeros_like(common)
    for bit in range(bits_of(SMALL)):
        parity ^= common >> bit & 1
    return np.kron(1 - 2 * parity, np.eye(FACTOR)).astype(jnp.bfloat16)


def butterflies(values):
    values = list(values)
    gap = 1
    while gap < len(values):
        for low in range(len(values)):
            if not low & gap:
                left, right = values[low], values[low | gap]
                values[low], values[low | gap] = left + right, left - right
        gap *= 2
    return values


def scaled(codes, scales):
    depth, cols = codes.shape
    groups = scales.shape[0]
    product = codes.astype(jnp.float32).reshape(groups, depth // groups, cols) * scales[:, None, :]
    return product.astype(jnp.bfloat16).reshape(depth, cols)


def fold_kernel(chunks, blocks, first, *refs):
    code_refs, (scale_in_ref, out_ref, scale_ref) = refs[:chunks], refs[chunks:]
    step = pl.program_id(0)

    @pl.when(step == 0)
    def _():
        scale_ref[...] = scale_in_ref[...].astype(jnp.float32)

    values = [
        code_refs[chunk][...].astype(jnp.float32) * scale_ref[pl.ds(chunk * blocks + first + step, 1), :]
        for chunk in range(chunks)
    ]
    for chunk, value in enumerate(butterflies(values)):
        out_ref[chunk] = value.astype(jnp.bfloat16)


def folded(down_code, down_scale, chunks, first, count):
    units, features = down_code.shape
    groups = down_scale.shape[0]
    blocks = groups // chunks
    depth = units // groups

    def code_spec(chunk):
        return pl.BlockSpec((depth, features), lambda k: (chunk * blocks + first + k, 0))

    return pl.pallas_call(
        functools.partial(fold_kernel, chunks, blocks, first),
        grid=(count,),
        in_specs=[code_spec(chunk) for chunk in range(chunks)]
        + [pl.BlockSpec((groups, features), lambda k: (0, 0))],
        out_specs=pl.BlockSpec((chunks, depth, features), lambda k: (0, k, 0)),
        out_shape=jax.ShapeDtypeStruct((chunks, count * depth, features), jnp.bfloat16),
        scratch_shapes=[pltpu.VMEM((groups, features), jnp.float32)],
        compiler_params=params(),
        cost_estimate=pl.CostEstimate(
            flops=0, bytes_accessed=4 * chunks * count * depth * features, transcendentals=0
        ),
        name=f"fold_down_{first}",
    )(*[down_code] * chunks, down_scale)


def gate_up_kernel(parts, peers, pieces, chunk, *refs):
    token_refs = refs[:parts]
    code_refs = refs[parts : parts + 2]
    scale_refs = refs[parts + 2 : parts + 4]
    keep_ref, send_ref, rows_ref, codes_ref, total_ref, terms_ref, arrived, done, left = refs[parts + 4 :]
    part = token_refs[0].shape[0]
    half, _, share, width = keep_ref.shape
    features = rows_ref.shape[1]
    depth = min(features, DEPTH)
    tiles = [(side, low) for side in range(2) for low in range(0, features, depth)]

    def fetch(index):
        side, low = tiles[index]
        return pltpu.make_async_copy(
            code_refs[side].at[pl.ds(low, depth), pl.ds(chunk * width, width)],
            codes_ref.at[side, pl.ds(low, depth), :],
            done.at[index],
        )

    def leave(side, which):
        return pltpu.make_async_copy(
            terms_ref.at[pl.ds(which * half, half), side],
            (keep_ref, send_ref)[which].at[:, side],
            left.at[side, which],
        )

    place = lax.axis_index("tensor")
    own = lax.axis_index("dp")
    piece_bits = bits_of(pieces)
    unit = min(part, share)
    fetch(0).start()
    placed = []
    for hop in range(peers):
        base = lax.rem(place + peers - hop, peers) * part
        for low in range(0, part, unit):
            row = base + low
            mixed = (row // share) ^ own
            piece = sum((mixed >> bit & 1) << (piece_bits - 1 - bit) for bit in range(piece_bits))
            slot = pl.multiple_of(piece * share + lax.rem(row, share), unit)

            def put(index, low=low, slot=slot, number=len(placed)):
                return pltpu.make_async_copy(
                    token_refs[index].at[pl.ds(low, unit), :],
                    rows_ref.at[pl.ds(slot, unit), :],
                    arrived.at[number],
                )

            placed.append(put(hop))
            placed[-1].start()
    for index in range(1, min(AHEAD, len(tiles))):
        fetch(index).start()
    for copy in placed:
        copy.wait()

    for index, (side, low) in enumerate(tiles):
        if index + AHEAD < len(tiles):
            fetch(index + AHEAD).start()
        fetch(index).wait()
        scales = scale_refs[side][...].astype(jnp.float32)
        group = features // scales.shape[0]
        weight = scaled(codes_ref[side, low : low + depth], scales[low // group : (low + depth) // group])
        terms = jnp.dot(rows_ref[:, low : low + depth], weight, preferred_element_type=jnp.float32)
        if low:
            terms = total_ref[...] + terms
        if low + depth < features:
            total_ref[...] = terms
            continue
        for piece in range(pieces):
            terms_ref[piece, side] = terms[piece * share : (piece + 1) * share].astype(jnp.bfloat16)
        for which in range(2):
            leave(side, which).start()
    for side in range(2):
        for which in range(2):
            leave(side, which).wait()


def gate_up(token_parts, gate_code, up_code, gate_scale, up_scale, chunk, width):
    peers = lax.axis_size("tensor")
    pieces = lax.axis_size("dp")
    part, features = token_parts[0].shape
    row_count = part * peers
    share = row_count // pieces
    groups = gate_scale.shape[0]
    out = jax.ShapeDtypeStruct((pieces // 2, 2, share, width), jnp.bfloat16)
    anywhere = pl.BlockSpec(memory_space=pl.ANY)
    return pl.pallas_call(
        functools.partial(gate_up_kernel, len(token_parts), peers, pieces, chunk),
        grid=(1,),
        in_specs=[anywhere] * (len(token_parts) + 2) + [pl.BlockSpec((groups, width), lambda k: (0, chunk))] * 2,
        out_specs=[anywhere, anywhere],
        out_shape=[out, out],
        scratch_shapes=[
            pltpu.VMEM((row_count, features), jnp.bfloat16),
            pltpu.VMEM((2, features, width), jnp.bfloat16),
            pltpu.VMEM((row_count, width), jnp.float32),
            pltpu.VMEM((pieces, 2, share, width), jnp.bfloat16),
            pltpu.SemaphoreType.DMA((row_count // min(part, share),)),
            pltpu.SemaphoreType.DMA((2 * features // min(features, DEPTH),)),
            pltpu.SemaphoreType.DMA((2, 2)),
        ],
        compiler_params=params(),
        cost_estimate=pl.CostEstimate(
            flops=4 * row_count * features * width, bytes_accessed=4 * features * width, transcendentals=0
        ),
        name=f"gate_up_{chunk}",
    )(*token_parts, gate_code, up_code, gate_scale, up_scale)


def hidden_kernel(count, *refs):
    sign_ref, rotation_ref, out_ref = refs[count:]
    total = sum(ref[0].astype(jnp.float32) for ref in refs[:count])
    gate, up = total[0], total[1]
    hidden = gate / (1.0 + jnp.exp(-gate)) * up * sign_ref[0]
    share, width = out_ref.shape
    small = rotation_ref.shape[0]
    slices = butterflies(hidden[:, low : low + small] for low in range(0, width, small))
    stacked = jnp.concatenate(slices, axis=0).astype(jnp.bfloat16)
    turned = jnp.dot(stacked, rotation_ref[...], preferred_element_type=jnp.float32) * POW**-0.5
    turned = [turned[index * share : (index + 1) * share] for index in range(len(slices))]
    out_ref[...] = jnp.concatenate(turned, axis=1).astype(jnp.bfloat16)


def hidden_of(terms, signs, rotation, chunk):
    _, _, share, width = terms[0].shape
    small = rotation.shape[0]
    return pl.pallas_call(
        functools.partial(hidden_kernel, len(terms)),
        grid=(1,),
        in_specs=[pl.BlockSpec((1, 2, share, width), lambda k: (0, 0, 0, 0))] * len(terms)
        + [pl.BlockSpec((1, 1, width), lambda k: (chunk, 0, 0)), pl.BlockSpec((small, small), lambda k: (0, 0))],
        out_specs=pl.BlockSpec((share, width), lambda k: (0, 0)),
        out_shape=jax.ShapeDtypeStruct((share, width), jnp.bfloat16),
        compiler_params=params(),
        cost_estimate=pl.CostEstimate(
            flops=2 * share * width * small, bytes_accessed=2 * share * width * 7, transcendentals=share * width
        ),
        name=f"hidden_{chunk}",
    )(*terms, signs, rotation)


def down_kernel(chunks, pieces, peers, sums, weights, outs, *refs):
    part_refs = refs[: chunks * pieces]
    weight_refs = refs[chunks * pieces : chunks * (pieces + weights)]
    sum_refs = refs[chunks * (pieces + weights) : chunks * (pieces + weights) + sums]
    out_refs, (rows_ref,) = refs[-1 - outs : -1], refs[-1:]
    share = part_refs[0].shape[0]
    row_count = share * pieces

    @pl.when(pl.program_id(0) == 0)
    def _():
        own = lax.axis_index("dp")
        place = lax.axis_index("tensor")
        part = row_count // peers
        for piece in range(pieces):
            block = own ^ reversed_bits(piece, bits_of(pieces))
            row = block * share
            turn = lax.rem(place + 2 * peers - 1 - row // part, peers)
            row = pl.multiple_of(turn * part + lax.rem(row, part), share)
            for chunk in range(chunks):
                rows_ref[chunk, pl.ds(row, share), :] = part_refs[chunk * pieces + piece][...]

    total = None
    for chunk in range(chunks):
        low = 0
        for weight_ref in weight_refs[chunk * weights : (chunk + 1) * weights]:
            high = low + weight_ref.shape[1]
            term = jnp.dot(rows_ref[chunk, :, low:high], weight_ref[0], preferred_element_type=jnp.float32)
            total = term if total is None else total + term
            low = high
    for sum_ref in sum_refs:
        total = total + sum_ref[...]
    size = row_count // outs
    for index, out_ref in enumerate(out_refs):
        out_ref[...] = total[index * size : (index + 1) * size].astype(out_ref.dtype)


def down(parts, weights, sums, chunk, column, columns, tile, kind, outs):
    peers = lax.axis_size("tensor")
    chunks, pieces = len(parts), len(parts[0])
    share, width = parts[0][0].shape
    row_count = share * pieces
    start = column * columns // tile

    def weight_spec(weight, index):
        return pl.BlockSpec((1, weight.shape[1], tile), lambda k: (index, 0, start + k))

    return pl.pallas_call(
        functools.partial(down_kernel, chunks, pieces, peers, len(sums), len(weights), outs),
        grid=(columns // tile,),
        in_specs=[pl.BlockSpec((share, width), lambda k: (0, 0))] * (chunks * pieces)
        + [weight_spec(weight, chunk + index) for index in range(chunks) for weight in weights]
        + [pl.BlockSpec((row_count, tile), lambda k: (0, start + k))] * len(sums),
        out_specs=[pl.BlockSpec((row_count // outs, tile), lambda k: (0, k))] * outs,
        out_shape=[jax.ShapeDtypeStruct((row_count // outs, columns), kind)] * outs,
        scratch_shapes=[pltpu.VMEM((chunks, row_count, width), jnp.bfloat16)],
        compiler_params=params(),
        cost_estimate=pl.CostEstimate(
            flops=2 * row_count * chunks * width * columns,
            bytes_accessed=2 * chunks * width * columns,
            transcendentals=0,
        ),
        name=f"down_{chunk}_{column}",
    )(*[piece for row in parts for piece in row], *weights * chunks, *sums)


def add(*terms):
    return sum(term.astype(jnp.float32) for term in terms).astype(jnp.bfloat16)


class Order:
    def __init__(self):
        self.last = None

    def __call__(self, step, operands):
        if self.last is not None:
            operands, _ = lax.optimization_barrier((operands, self.last))
        result = step(operands)
        self.last = jax.tree.leaves(result)[0]
        return result

    def land(self, value):
        value, self.last = lax.optimization_barrier((value, self.last))
        return value


def upper(terms):
    half = terms[0].shape[0] // 2
    return add(*[term[half : 2 * half] for term in terms])


def lower(terms):
    half = terms[0].shape[0] // 2
    return [term[:half] for term in terms] if half > 1 else terms


def doubled(hidden, axis):
    parts = [hidden]
    for bit in reversed(range(bits_of(lax.axis_size(axis)))):
        parts = parts + [swap(part, axis, bit) for part in parts]
    return parts


def on_device(tokens, gate_code, up_code, down_code, gate_scale, up_scale, down_scale, sign_bits):
    peers = lax.axis_size("tensor")
    dp_bits = bits_of(lax.axis_size("dp"))
    turns = bits_of(peers)
    width = LOW * FACTOR
    chunks = gate_code.shape[1] // width
    rotation = jnp.asarray(matrix_part())
    signs = (2.0 * sign_bits.astype(jnp.float32) - 1.0).reshape(chunks, 1, width)
    place = lax.axis_index("tensor")
    features = down_code.shape[1]
    blocks = down_scale.shape[0] // chunks
    order = Order()
    weights = []
    all_terms = {}
    hiddens = {}
    parts = {}

    def fold(count):
        first = sum(weight.shape[1] for weight in weights) * chunks * down_scale.shape[0] // down_code.shape[0]
        first //= chunks
        weights.append(order(lambda codes: folded(codes, down_scale, chunks, first, count), down_code))

    def start_terms(chunk):
        keep, send = order(
            lambda ts: gate_up(ts, gate_code, up_code, gate_scale, up_scale, chunk, width), token_parts
        )
        all_terms[chunk] = [keep, swap(send, "dp", 0)]

    def pass_terms(chunk, bit=1):
        terms = all_terms[chunk]
        send = order(upper, terms)
        all_terms[chunk] = lower(terms) + [swap(send, "dp", bit)]

    def finish_terms(chunk):
        hidden = order(lambda ts: hidden_of(ts, signs, rotation, chunk), all_terms[chunk])
        hiddens[chunk] = hidden, swap(hidden, "tensor", 0)

    def turn(chunk, bit):
        sign = (1 - 2 * (place >> bit & 1)).astype(jnp.float32)
        hidden = order(lambda pair: add(pair[1], sign * pair[0].astype(jnp.float32)), hiddens[chunk])
        if bit + 1 < turns:
            hiddens[chunk] = hidden, swap(hidden, "tensor", bit + 1)
        else:
            parts[chunk] = doubled(hidden, "dp")

    def product(first, count, sums, column, columns, kind, outs):
        given = [parts[chunk] for chunk in range(first, first + count)]
        tile = min(columns, 512)
        return order(lambda ps: down(ps, weights, sums, first, column, columns, tile, kind, outs), given)

    def finish(first, count, sums, halves=2):
        columns = features // halves
        totals = []
        if peers == 4:
            for column in range(halves):
                behind, far, before, own = product(first, count, sums, column, columns, jnp.bfloat16, peers)
                totals.append(
                    [own, shift(far, "tensor", 2), shift(behind, "tensor", -1), shift(before, "tensor")]
                )
            totals = [order(lambda ts: add(*ts), total) for total in totals]
            return jnp.concatenate(totals, axis=1)
        terms = []
        for column in range(halves):
            terms.append(product(first, count, sums, column, columns, jnp.bfloat16, peers))
            totals.append(shift(terms[-1][0], "tensor"))
        for hop in range(1, peers):
            for column in range(halves):
                totals[column] = order(lambda pair: add(*pair), (totals[column], terms[column][hop]))
                if hop < peers - 1:
                    totals[column] = shift(totals[column], "tensor")
        return jnp.concatenate(totals, axis=1)

    token_parts = [tokens] + [shift(tokens, "tensor", hop) for hop in range(1, peers)]
    token_parts = list(lax.optimization_barrier(tuple(token_parts)))
    fold(min(blocks, FOLD))
    rest = blocks - sum(weight.shape[1] for weight in weights) * down_scale.shape[0] // down_code.shape[0]

    def land_terms(chunk):
        all_terms[chunk][-1] = order.land(all_terms[chunk][-1])

    def land_turn(chunk):
        hidden, partner = hiddens[chunk]
        hiddens[chunk] = hidden, order.land(partner)

    def land_parts(chunk):
        parts[chunk][1:] = order.land(parts[chunk][1:])

    if chunks == 4 and dp_bits == 2 and turns == 2:
        start_terms(0)
        start_terms(1)
        land_terms(0)
        pass_terms(0)
        start_terms(2)
        land_terms(0)
        land_terms(1)
        pass_terms(1)
        finish_terms(0)
        start_terms(3)
        land_turn(0)
        land_terms(1)
        land_terms(2)
        pass_terms(2)
        turn(0, 0)
        finish_terms(1)
        land_terms(3)
        pass_terms(3)
        fold(rest // 2)
        land_terms(2)
        finish_terms(2)
        land_turn(1)
        turn(1, 0)
        land_turn(0)
        turn(0, 1)
        fold(rest - rest // 2)
        land_turn(2)
        land_terms(3)
        finish_terms(3)
        turn(2, 0)
        land_turn(1)
        turn(1, 1)
        land_parts(0)
        sums = product(0, 1, [], 0, features, jnp.float32, 1)
        land_turn(3)
        turn(3, 0)
        land_turn(2)
        turn(2, 1)
        land_parts(1)
        sums = product(1, 1, sums, 0, features, jnp.float32, 1)
        land_turn(3)
        turn(3, 1)
        return finish(2, 2, sums)
    fold(rest)
    for chunk in range(chunks):
        start_terms(chunk)
        for bit in range(1, dp_bits):
            pass_terms(chunk, bit)
        finish_terms(chunk)
        for bit in range(turns):
            turn(chunk, bit)
    return finish(0, chunks, [])


def solution(mesh):
    in_specs = (
        P(("groups", "tensor"), "dp"),
        P("dp", "tensor"),
        P("dp", "tensor"),
        P("tensor", "dp"),
        P("dp", "tensor"),
        P("dp", "tensor"),
        P("tensor", "dp"),
        P("tensor"),
    )
    out_specs = P(("groups", "tensor"), "dp")
    return jax.shard_map(
        on_device, mesh=mesh, in_specs=in_specs, out_specs=out_specs, check_vma=False
    )
```

```python
import functools

import jax
import jax.numpy as jnp
import numpy as np
from jax import lax
from jax.experimental import pallas as pl
from jax.experimental.pallas import tpu as pltpu
from jax.sharding import PartitionSpec as P

POW = 2048
FACTOR = 13
LOW = 128
SMALL = 16
FOLD = 8
DEPTH = 1024
AHEAD = 2
VMEM_LIMIT = 32 * 2**20


def bits_of(size):
    return size.bit_length() - 1


def swap(shard, axis, bit):
    return lax.ppermute(shard, axis, [(i, i ^ 1 << bit) for i in range(lax.axis_size(axis))])


def shift(shard, axis, step=1):
    size = lax.axis_size(axis)
    return lax.ppermute(shard, axis, [(i, (i + step) % size) for i in range(size)])


def reversed_bits(value, bits):
    return sum((value >> i & 1) << (bits - 1 - i) for i in range(bits))


def params(**more):
    return pltpu.CompilerParams(vmem_limit_bytes=VMEM_LIMIT, **more)


def matrix_part():
    order = np.arange(SMALL)
    common = order[:, None] & order[None, :]
    parity = np.zeros_like(common)
    for bit in range(bits_of(SMALL)):
        parity ^= common >> bit & 1
    return np.kron(1 - 2 * parity, np.eye(FACTOR)).astype(jnp.bfloat16)


def butterflies(values):
    values = list(values)
    gap = 1
    while gap < len(values):
        for low in range(len(values)):
            if not low & gap:
                left, right = values[low], values[low | gap]
                values[low], values[low | gap] = left + right, left - right
        gap *= 2
    return values


def scaled(codes, scales):
    depth, cols = codes.shape
    groups = scales.shape[0]
    product = codes.astype(jnp.float32).reshape(groups, depth // groups, cols) * scales[:, None, :]
    return product.astype(jnp.bfloat16).reshape(depth, cols)


def fold_kernel(chunks, blocks, first, *refs):
    code_refs, (scale_in_ref, out_ref, scale_ref) = refs[:chunks], refs[chunks:]
    step = pl.program_id(0)

    @pl.when(step == 0)
    def _():
        scale_ref[...] = scale_in_ref[...].astype(jnp.float32)

    values = [
        code_refs[chunk][...].astype(jnp.float32) * scale_ref[pl.ds(chunk * blocks + first + step, 1), :]
        for chunk in range(chunks)
    ]
    for chunk, value in enumerate(butterflies(values)):
        out_ref[chunk] = value.astype(jnp.bfloat16)


def folded(down_code, down_scale, chunks, first, count):
    units, features = down_code.shape
    groups = down_scale.shape[0]
    blocks = groups // chunks
    depth = units // groups

    def code_spec(chunk):
        return pl.BlockSpec((depth, features), lambda k: (chunk * blocks + first + k, 0))

    return pl.pallas_call(
        functools.partial(fold_kernel, chunks, blocks, first),
        grid=(count,),
        in_specs=[code_spec(chunk) for chunk in range(chunks)]
        + [pl.BlockSpec((groups, features), lambda k: (0, 0))],
        out_specs=pl.BlockSpec((chunks, depth, features), lambda k: (0, k, 0)),
        out_shape=jax.ShapeDtypeStruct((chunks, count * depth, features), jnp.bfloat16),
        scratch_shapes=[pltpu.VMEM((groups, features), jnp.float32)],
        compiler_params=params(),
        cost_estimate=pl.CostEstimate(
            flops=0, bytes_accessed=4 * chunks * count * depth * features, transcendentals=0
        ),
        name=f"fold_down_{first}",
    )(*[down_code] * chunks, down_scale)


def gate_up_kernel(parts, peers, pieces, chunk, *refs):
    token_refs = refs[:parts]
    code_refs = refs[parts : parts + 2]
    scale_refs = refs[parts + 2 : parts + 4]
    keep_ref, send_ref, rows_ref, codes_ref, total_ref, terms_ref, arrived, done, left = refs[parts + 4 :]
    part = token_refs[0].shape[0]
    half, _, share, width = keep_ref.shape
    features = rows_ref.shape[1]
    depth = min(features, DEPTH)
    tiles = [(side, low) for side in range(2) for low in range(0, features, depth)]

    def fetch(index):
        side, low = tiles[index]
        return pltpu.make_async_copy(
            code_refs[side].at[pl.ds(low, depth), pl.ds(chunk * width, width)],
            codes_ref.at[side, pl.ds(low, depth), :],
            done.at[index],
        )

    def leave(side, which):
        return pltpu.make_async_copy(
            terms_ref.at[pl.ds(which * half, half), side],
            (keep_ref, send_ref)[which].at[:, side],
            left.at[side, which],
        )

    place = lax.axis_index("tensor")
    own = lax.axis_index("dp")
    piece_bits = bits_of(pieces)
    unit = min(part, share)
    fetch(0).start()
    placed = []
    for hop in range(peers):
        base = lax.rem(place + peers - hop, peers) * part
        for low in range(0, part, unit):
            row = base + low
            mixed = (row // share) ^ own
            piece = sum((mixed >> bit & 1) << (piece_bits - 1 - bit) for bit in range(piece_bits))
            slot = pl.multiple_of(piece * share + lax.rem(row, share), unit)

            def put(index, low=low, slot=slot, number=len(placed)):
                return pltpu.make_async_copy(
                    token_refs[index].at[pl.ds(low, unit), :],
                    rows_ref.at[pl.ds(slot, unit), :],
                    arrived.at[number],
                )

            placed.append(put(hop))
            placed[-1].start()
    for index in range(1, min(AHEAD, len(tiles))):
        fetch(index).start()
    for copy in placed:
        copy.wait()

    for index, (side, low) in enumerate(tiles):
        if index + AHEAD < len(tiles):
            fetch(index + AHEAD).start()
        fetch(index).wait()
        scales = scale_refs[side][...].astype(jnp.float32)
        group = features // scales.shape[0]
        weight = scaled(codes_ref[side, low : low + depth], scales[low // group : (low + depth) // group])
        terms = jnp.dot(rows_ref[:, low : low + depth], weight, preferred_element_type=jnp.float32)
        if low:
            terms = total_ref[...] + terms
        if low + depth < features:
            total_ref[...] = terms
            continue
        for piece in range(pieces):
            terms_ref[piece, side] = terms[piece * share : (piece + 1) * share].astype(jnp.bfloat16)
        for which in range(2):
            leave(side, which).start()
    for side in range(2):
        for which in range(2):
            leave(side, which).wait()


def gate_up(token_parts, gate_code, up_code, gate_scale, up_scale, chunk, width):
    peers = lax.axis_size("tensor")
    pieces = lax.axis_size("dp")
    part, features = token_parts[0].shape
    row_count = part * peers
    share = row_count // pieces
    groups = gate_scale.shape[0]
    out = jax.ShapeDtypeStruct((pieces // 2, 2, share, width), jnp.bfloat16)
    anywhere = pl.BlockSpec(memory_space=pl.ANY)
    return pl.pallas_call(
        functools.partial(gate_up_kernel, len(token_parts), peers, pieces, chunk),
        grid=(1,),
        in_specs=[anywhere] * (len(token_parts) + 2) + [pl.BlockSpec((groups, width), lambda k: (0, chunk))] * 2,
        out_specs=[anywhere, anywhere],
        out_shape=[out, out],
        scratch_shapes=[
            pltpu.VMEM((row_count, features), jnp.bfloat16),
            pltpu.VMEM((2, features, width), jnp.bfloat16),
            pltpu.VMEM((row_count, width), jnp.float32),
            pltpu.VMEM((pieces, 2, share, width), jnp.bfloat16),
            pltpu.SemaphoreType.DMA((row_count // min(part, share),)),
            pltpu.SemaphoreType.DMA((2 * features // min(features, DEPTH),)),
            pltpu.SemaphoreType.DMA((2, 2)),
        ],
        compiler_params=params(),
        cost_estimate=pl.CostEstimate(
            flops=4 * row_count * features * width, bytes_accessed=4 * features * width, transcendentals=0
        ),
        name=f"gate_up_{chunk}",
    )(*token_parts, gate_code, up_code, gate_scale, up_scale)


def hidden_kernel(count, *refs):
    sign_ref, rotation_ref, out_ref = refs[count:]
    total = sum(ref[0].astype(jnp.float32) for ref in refs[:count])
    gate, up = total[0], total[1]
    hidden = gate / (1.0 + jnp.exp(-gate)) * up * sign_ref[0]
    share, width = out_ref.shape
    small = rotation_ref.shape[0]
    slices = butterflies(hidden[:, low : low + small] for low in range(0, width, small))
    stacked = jnp.concatenate(slices, axis=0).astype(jnp.bfloat16)
    turned = jnp.dot(stacked, rotation_ref[...], preferred_element_type=jnp.float32) * POW**-0.5
    turned = [turned[index * share : (index + 1) * share] for index in range(len(slices))]
    out_ref[...] = jnp.concatenate(turned, axis=1).astype(jnp.bfloat16)


def hidden_of(terms, signs, rotation, chunk):
    _, _, share, width = terms[0].shape
    small = rotation.shape[0]
    return pl.pallas_call(
        functools.partial(hidden_kernel, len(terms)),
        grid=(1,),
        in_specs=[pl.BlockSpec((1, 2, share, width), lambda k: (0, 0, 0, 0))] * len(terms)
        + [pl.BlockSpec((1, 1, width), lambda k: (chunk, 0, 0)), pl.BlockSpec((small, small), lambda k: (0, 0))],
        out_specs=pl.BlockSpec((share, width), lambda k: (0, 0)),
        out_shape=jax.ShapeDtypeStruct((share, width), jnp.bfloat16),
        compiler_params=params(),
        cost_estimate=pl.CostEstimate(
            flops=2 * share * width * small, bytes_accessed=2 * share * width * 7, transcendentals=share * width
        ),
        name=f"hidden_{chunk}",
    )(*terms, signs, rotation)


def down_kernel(chunks, pieces, peers, sums, weights, outs, *refs):
    part_refs = refs[: chunks * pieces]
    weight_refs = refs[chunks * pieces : chunks * (pieces + weights)]
    sum_refs = refs[chunks * (pieces + weights) : chunks * (pieces + weights) + sums]
    out_refs, (rows_ref,) = refs[-1 - outs : -1], refs[-1:]
    share = part_refs[0].shape[0]
    row_count = share * pieces

    @pl.when(pl.program_id(0) == 0)
    def _():
        own = lax.axis_index("dp")
        place = lax.axis_index("tensor")
        part = row_count // peers
        for piece in range(pieces):
            block = own ^ reversed_bits(piece, bits_of(pieces))
            row = block * share
            turn = lax.rem(place + 2 * peers - 1 - row // part, peers)
            row = pl.multiple_of(turn * part + lax.rem(row, part), share)
            for chunk in range(chunks):
                rows_ref[chunk, pl.ds(row, share), :] = part_refs[chunk * pieces + piece][...]

    total = None
    for chunk in range(chunks):
        low = 0
        for weight_ref in weight_refs[chunk * weights : (chunk + 1) * weights]:
            high = low + weight_ref.shape[1]
            term = jnp.dot(rows_ref[chunk, :, low:high], weight_ref[0], preferred_element_type=jnp.float32)
            total = term if total is None else total + term
            low = high
    for sum_ref in sum_refs:
        total = total + sum_ref[...]
    size = row_count // outs
    for index, out_ref in enumerate(out_refs):
        out_ref[...] = total[index * size : (index + 1) * size].astype(out_ref.dtype)


def down(parts, weights, sums, chunk, column, columns, tile, kind, outs):
    peers = lax.axis_size("tensor")
    chunks, pieces = len(parts), len(parts[0])
    share, width = parts[0][0].shape
    row_count = share * pieces
    start = column * columns // tile

    def weight_spec(weight, index):
        return pl.BlockSpec((1, weight.shape[1], tile), lambda k: (index, 0, start + k))

    return pl.pallas_call(
        functools.partial(down_kernel, chunks, pieces, peers, len(sums), len(weights), outs),
        grid=(columns // tile,),
        in_specs=[pl.BlockSpec((share, width), lambda k: (0, 0))] * (chunks * pieces)
        + [weight_spec(weight, chunk + index) for index in range(chunks) for weight in weights]
        + [pl.BlockSpec((row_count, tile), lambda k: (0, start + k))] * len(sums),
        out_specs=[pl.BlockSpec((row_count // outs, tile), lambda k: (0, k))] * outs,
        out_shape=[jax.ShapeDtypeStruct((row_count // outs, columns), kind)] * outs,
        scratch_shapes=[pltpu.VMEM((chunks, row_count, width), jnp.bfloat16)],
        compiler_params=params(),
        cost_estimate=pl.CostEstimate(
            flops=2 * row_count * chunks * width * columns,
            bytes_accessed=2 * chunks * width * columns,
            transcendentals=0,
        ),
        name=f"down_{chunk}_{column}",
    )(*[piece for row in parts for piece in row], *weights * chunks, *sums)


def add(*terms):
    return sum(term.astype(jnp.float32) for term in terms).astype(jnp.bfloat16)


class Order:
    def __init__(self):
        self.last = None

    def __call__(self, step, operands):
        if self.last is not None:
            operands, _ = lax.optimization_barrier((operands, self.last))
        result = step(operands)
        self.last = jax.tree.leaves(result)[0]
        return result

    def land(self, value):
        value, self.last = lax.optimization_barrier((value, self.last))
        return value


def upper(terms):
    half = terms[0].shape[0] // 2
    return add(*[term[half : 2 * half] for term in terms])


def lower(terms):
    half = terms[0].shape[0] // 2
    return [term[:half] for term in terms] if half > 1 else terms


def doubled(hidden, axis):
    parts = [hidden]
    for bit in reversed(range(bits_of(lax.axis_size(axis)))):
        parts = parts + [swap(part, axis, bit) for part in parts]
    return parts


def on_device(tokens, gate_code, up_code, down_code, gate_scale, up_scale, down_scale, sign_bits):
    peers = lax.axis_size("tensor")
    dp_bits = bits_of(lax.axis_size("dp"))
    turns = bits_of(peers)
    width = LOW * FACTOR
    chunks = gate_code.shape[1] // width
    rotation = jnp.asarray(matrix_part())
    signs = (2.0 * sign_bits.astype(jnp.float32) - 1.0).reshape(chunks, 1, width)
    place = lax.axis_index("tensor")
    features = down_code.shape[1]
    blocks = down_scale.shape[0] // chunks
    order = Order()
    weights = []
    all_terms = {}
    hiddens = {}
    parts = {}

    def fold(count):
        first = sum(weight.shape[1] for weight in weights) * chunks * down_scale.shape[0] // down_code.shape[0]
        first //= chunks
        weights.append(order(lambda codes: folded(codes, down_scale, chunks, first, count), down_code))

    def start_terms(chunk):
        keep, send = order(
            lambda ts: gate_up(ts, gate_code, up_code, gate_scale, up_scale, chunk, width), token_parts
        )
        all_terms[chunk] = [keep, swap(send, "dp", 0)]

    def pass_terms(chunk, bit=1):
        terms = all_terms[chunk]
        send = order(upper, terms)
        all_terms[chunk] = lower(terms) + [swap(send, "dp", bit)]

    def finish_terms(chunk):
        hidden = order(lambda ts: hidden_of(ts, signs, rotation, chunk), all_terms[chunk])
        hiddens[chunk] = hidden, swap(hidden, "tensor", 0)

    def turn(chunk, bit):
        sign = (1 - 2 * (place >> bit & 1)).astype(jnp.float32)
        hidden = order(lambda pair: add(pair[1], sign * pair[0].astype(jnp.float32)), hiddens[chunk])
        if bit + 1 < turns:
            hiddens[chunk] = hidden, swap(hidden, "tensor", bit + 1)
        else:
            parts[chunk] = doubled(hidden, "dp")

    def product(first, count, sums, column, columns, kind, outs):
        given = [parts[chunk] for chunk in range(first, first + count)]
        tile = min(columns, 512)
        return order(lambda ps: down(ps, weights, sums, first, column, columns, tile, kind, outs), given)

    def finish(first, count, sums, halves=2):
        columns = features // halves
        totals = []
        if peers == 4:
            for column in range(halves):
                behind, far, before, own = product(first, count, sums, column, columns, jnp.bfloat16, peers)
                totals.append(
                    [own, shift(far, "tensor", 2), shift(behind, "tensor", -1), shift(before, "tensor")]
                )
            totals = [order(lambda ts: add(*ts), total) for total in totals]
            return jnp.concatenate(totals, axis=1)
        terms = []
        for column in range(halves):
            terms.append(product(first, count, sums, column, columns, jnp.bfloat16, peers))
            totals.append(shift(terms[-1][0], "tensor"))
        for hop in range(1, peers):
            for column in range(halves):
                totals[column] = order(lambda pair: add(*pair), (totals[column], terms[column][hop]))
                if hop < peers - 1:
                    totals[column] = shift(totals[column], "tensor")
        return jnp.concatenate(totals, axis=1)

    token_parts = [tokens] + [shift(tokens, "tensor", hop) for hop in range(1, peers)]
    token_parts = list(lax.optimization_barrier(tuple(token_parts)))
    fold(min(blocks, FOLD))
    rest = blocks - sum(weight.shape[1] for weight in weights) * down_scale.shape[0] // down_code.shape[0]

    def land_terms(chunk):
        all_terms[chunk][-1] = order.land(all_terms[chunk][-1])

    def land_turn(chunk):
        hidden, partner = hiddens[chunk]
        hiddens[chunk] = hidden, order.land(partner)

    def land_parts(chunk):
        parts[chunk][1:] = order.land(parts[chunk][1:])

    if chunks == 4 and dp_bits == 2 and turns == 2:
        start_terms(0)
        start_terms(1)
        land_terms(0)
        pass_terms(0)
        start_terms(2)
        land_terms(0)
        land_terms(1)
        pass_terms(1)
        finish_terms(0)
        start_terms(3)
        land_terms(1)
        land_terms(2)
        pass_terms(2)
        finish_terms(1)
        land_turn(0)
        turn(0, 0)
        land_terms(3)
        pass_terms(3)
        fold(rest)
        land_turn(1)
        turn(1, 0)
        land_terms(2)
        finish_terms(2)
        land_turn(0)
        turn(0, 1)
        land_terms(3)
        finish_terms(3)
        land_turn(2)
        turn(2, 0)
        land_parts(0)
        sums = product(0, 1, [], 0, features, jnp.float32, 1)
        land_turn(1)
        turn(1, 1)
        land_turn(3)
        turn(3, 0)
        land_turn(2)
        turn(2, 1)
        land_parts(1)
        sums = product(1, 1, sums, 0, features, jnp.float32, 1)
        land_turn(3)
        turn(3, 1)
        return finish(2, 2, sums)
    fold(rest)
    for chunk in range(chunks):
        start_terms(chunk)
        for bit in range(1, dp_bits):
            pass_terms(chunk, bit)
        finish_terms(chunk)
        for bit in range(turns):
            turn(chunk, bit)
    return finish(0, chunks, [])


def solution(mesh):
    in_specs = (
        P(("groups", "tensor"), "dp"),
        P("dp", "tensor"),
        P("dp", "tensor"),
        P("tensor", "dp"),
        P("dp", "tensor"),
        P("dp", "tensor"),
        P("tensor", "dp"),
        P("tensor"),
    )
    out_specs = P(("groups", "tensor"), "dp")
    return jax.shard_map(
        on_device, mesh=mesh, in_specs=in_specs, out_specs=out_specs, check_vma=False
    )
```
